256 devices in a mesh: island: 8 (over y, x_lo), tp: 32 (over x_hi, z, core).
Axes of the slice: x: 4 (x_hi: 2, x_lo: 2; x = x_hi * 2 + x_lo), y: 4, z: 8, core: 2. Of those that a mesh axis runs over, the one named last changes fastest.
Arguments:
- query: bfloat16 [8192, 4096], P('island', 'tp'), may hold values from -5 to 5
- key: bfloat16 [8192, 4096], P('island', 'tp'), may hold values from -5 to 5
- value: bfloat16 [8192, 4096], P('island', 'tp'), may hold values from -6 to 6
- resid: bfloat16 [8192, 4096], P(('island', 'tp')), may hold values from -6 to 6
- w_out: bfloat16 [8, 4096, 4096], P('island', 'tp'), may hold values from -0.09375 to 0.09375
- gain: bfloat16 [8, 4096], P('island'), may hold values from 0.5 to 1.5
- grad_norm: bfloat16 [8192, 4096], P(('island', 'tp')), may hold values from -0.59765625 to 0.59765625
- grad_resid: bfloat16 [8192, 4096], P(('island', 'tp')), may hold values from -0.59765625 to 0.59765625
- moment_one: bfloat16 [8, 4096, 4096], P('island', 'tp'), may hold values from -18 to 18
- moment_two: bfloat16 [8, 4096, 4096], P('island', 'tp'), may hold values from 2 to 50
- delta: bfloat16 [8, 4096, 4096], P('island', 'tp'), may hold values from -0.059814453 to 0.059814453
- global_w: float32 [4096, 4096], P('tp', 'island'), may hold values from -0.09375 to 0.09375
- momentum: float32 [4096, 4096], P('tp', 'island'), may hold values from -0.06 to 0.06
Outputs:
- hidden: bfloat16 [8192, 4096], P(('island', 'tp'))
- grad_query: bfloat16 [8192, 4096], P('island', 'tp')
- grad_key: bfloat16 [8192, 4096], P('island', 'tp')
- grad_value: bfloat16 [8192, 4096], P('island', 'tp')
- new_w_out: bfloat16 [8, 4096, 4096], P('island', 'tp')
- new_moment_one: bfloat16 [8, 4096, 4096], P('island', 'tp')
- new_moment_two: bfloat16 [8, 4096, 4096], P('island', 'tp')
- new_global: float32 [4096, 4096], P('tp', 'island')
- new_momentum: float32 [4096, 4096], P('tp', 'island')
- fragment_params: bfloat16 [4096, 4096], P('tp')
The draws below stay inside these ranges and needn't reach their ends.
All inputs are finite; a program needn't handle non-finite values.
Results may differ from the reference program's by a relative error of at most 0.03.
Values may be sent and summed in bfloat16 or wider, within the bound.
A program may use at most 128 MiB of HBM per device.

```python
import math
import jax
import jax.numpy as jnp
from jax import lax

D = 4096
HEAD = 128
HEADS = 32
TOKENS = 1024
WIDTH_HEADS = 4096
ALL_TOK = 8192
N_ISLAND = 8
N_TP = 32


def draw_query(key, part):
    key = jax.random.fold_in(key, 1)
    values = jnp.clip(jax.random.normal(key, (ALL_TOK, WIDTH_HEADS), jnp.float32), -5.0, 5.0)
    return values.astype(jnp.bfloat16)


def draw_key(key, part):
    key = jax.random.fold_in(key, 2)
    values = jnp.clip(jax.random.normal(key, (ALL_TOK, WIDTH_HEADS), jnp.float32), -5.0, 5.0)
    return values.astype(jnp.bfloat16)


def strengthened(values, own_key, source, target, parts, factor):
    def block_of(axis_at):
        return (jnp.arange(values.shape[axis_at]) // (values.shape[axis_at] // parts)).reshape((-1,) + (1,) * (values.ndim - 1 - axis_at))

    near = jax.random.permutation(own_key, parts)[block_of(target)]
    far = (block_of(target) + parts // 2) % parts
    return jnp.where((block_of(source) == near) | (block_of(source) == far), factor * values, values)


def block_scale(stream_key, dims, pieces, least, largest):
    def one(position, blocks):
        draws = jax.random.uniform(jax.random.fold_in(jax.random.fold_in(stream_key, 6), position), (blocks,), jnp.float32, least / len(pieces), largest / len(pieces))
        return jnp.repeat(jnp.exp(draws), dims[position] // blocks).reshape((-1,) + (1,) * (len(dims) - position - 1))

    loudness = one(*pieces[0])
    for cut in pieces[1:]:
        loudness = loudness * one(*cut)
    return loudness


def scatter_about(key, dims, scale, reach, pieces=(), kind=jnp.bfloat16):
    level = block_scale(key, dims, pieces, -0.22, 0.18) if pieces else 1.0
    result = jax.random.normal(key, dims, jnp.float32) * scale * level
    return jnp.minimum(jnp.maximum(result, -reach), reach).astype(kind)


def noise_with(rng, dims, width, reach, cuts, heavy, held_as=jnp.bfloat16):
    values = width * jax.random.normal(rng, dims, jnp.float32)
    if cuts:
        values = values * block_scale(rng, dims, cuts, -0.22, 0.18)
    return jnp.clip(strengthened(values, jax.random.fold_in(rng, 3), *heavy), -reach, reach).astype(held_as)


def setup_inputs(seed: int = 0) -> dict:
    key_of = jax.random.split(jax.random.key(seed), 14)
    query = draw_query(jax.random.fold_in(key_of[13], 71), 0)
    key = draw_key(jax.random.fold_in(key_of[13], 71), 0)
    value = scatter_about(key_of[2], (ALL_TOK, WIDTH_HEADS), 1.0, 6.0, ((0, 8), (1, 32)))
    resid = scatter_about(key_of[3], (ALL_TOK, D), 1.0, 6.0, ((0, 256),))
    w_out = scatter_about(key_of[4], (N_ISLAND, WIDTH_HEADS, D), WIDTH_HEADS ** -0.5, 0.09375, ((0, 8), (1, 32)))
    gain = jnp.clip(1.0 + 0.1 * jax.random.normal(key_of[5], (N_ISLAND, D), jnp.float32), 0.5, 1.5).astype(jnp.bfloat16)
    grad_norm = scatter_about(key_of[6], (ALL_TOK, D), 0.1, 0.59765625, ((0, 256),))
    grad_resid = scatter_about(key_of[7], (ALL_TOK, D), 0.1, 0.59765625, ((0, 256),))
    moment_one = scatter_about(key_of[8], (N_ISLAND, WIDTH_HEADS, D), 3.0, 18.0, ((0, 8), (1, 32)))
    moment_two = jnp.clip(jnp.exp(math.log(50.0) - 3.218876 * jax.random.uniform(key_of[9], (N_ISLAND, WIDTH_HEADS, D), jnp.float32) ** block_scale(key_of[9], (N_ISLAND, WIDTH_HEADS, D), ((0, 8), (1, 32)), -0.2, 0.2)), 2.0, 50.0).astype(jnp.bfloat16)
    delta = noise_with(key_of[10], (N_ISLAND, WIDTH_HEADS, D), 0.01, 0.059814453, ((0, 8), (1, 32)), (0, 2, 8, 2.0))
    global_w = scatter_about(key_of[11], (WIDTH_HEADS, D), D ** -0.5, 0.09375, ((0, 32), (1, 8)), jnp.float32)
    momentum = scatter_about(key_of[12], (WIDTH_HEADS, D), 0.01, 0.06, ((0, 32), (1, 8)), jnp.float32)
    return dict(query=query, key=key, value=value, resid=resid, w_out=w_out, gain=gain, grad_norm=grad_norm, grad_resid=grad_resid, moment_one=moment_one, moment_two=moment_two, delta=delta, global_w=global_w, momentum=momentum)


def norm_back(hidden, gain_row, grad_norm, grad_resid):
    values = hidden.astype(jnp.float32)
    rstd = lax.rsqrt(lax.optimization_barrier(jnp.mean(values * values, axis=1, keepdims=True)) + 1e-05)
    normed = values * rstd
    scaled = grad_norm.astype(jnp.float32) * gain_row.astype(jnp.float32)[None, :]
    inner = lax.optimization_barrier(jnp.mean(scaled * normed, axis=1, keepdims=True))
    back = grad_resid.astype(jnp.float32) + rstd * (scaled - normed * inner)
    return back.astype(jnp.bfloat16)

def attention_probs(queries, keys):
    scale = HEAD ** (-0.5)
    scores = jnp.einsum('qhd,khd->hqk', queries.astype(jnp.float32), keys.astype(jnp.float32)) * scale
    qpos = lax.broadcasted_iota(jnp.int32, (TOKENS, TOKENS), 0)
    kpos = lax.broadcasted_iota(jnp.int32, (TOKENS, TOKENS), 1)
    scores = jnp.where((kpos <= qpos)[None], scores, -1e+30)
    top = lax.optimization_barrier(jnp.max(scores, axis=2, keepdims=True))
    expo = jnp.exp(scores - top)
    return expo / lax.optimization_barrier(jnp.sum(expo, axis=2, keepdims=True))

def replica_step(query, key, value, resid, weight, gain_row, grad_norm, grad_resid, first_in, second_in):
    scale = HEAD ** (-0.5)
    queries = query.reshape(TOKENS, HEADS, HEAD)
    keys = key.reshape(TOKENS, HEADS, HEAD)
    values = value.reshape(TOKENS, HEADS, HEAD)
    probs32 = attention_probs(queries, keys)
    probs = probs32.astype(jnp.bfloat16)
    context3 = jnp.einsum('hqk,khd->qhd', probs.astype(jnp.float32), values.astype(jnp.float32)).astype(jnp.bfloat16)
    context = context3.reshape(TOKENS, WIDTH_HEADS)
    group = WIDTH_HEADS // N_TP
    ctx_groups = context.reshape(TOKENS, N_TP, group).transpose(1, 0, 2)
    w_groups = weight.reshape(N_TP, group, D)

    def add_group(total, pair):
        part = jnp.dot(pair[0], pair[1], preferred_element_type=jnp.float32).astype(jnp.bfloat16)
        return (total + part.astype(jnp.float32), None)
    summed, _ = lax.scan(add_group, jnp.zeros((TOKENS, D), jnp.float32), (ctx_groups, w_groups))
    hidden = (resid.astype(jnp.float32) + summed).astype(jnp.bfloat16)
    grad_hidden = norm_back(hidden, gain_row, grad_norm, grad_resid)
    grad_w = lax.dot_general(context, grad_hidden, (((0,), (0,)), ((), ())), preferred_element_type=jnp.float32)
    grad_context = lax.dot_general(grad_hidden, weight, (((1,), (1,)), ((), ())), preferred_element_type=jnp.float32).astype(jnp.bfloat16)
    grad_ctx32 = grad_context.reshape(TOKENS, HEADS, HEAD).astype(jnp.float32)
    grad_probs = jnp.einsum('qhd,khd->hqk', grad_ctx32, values.astype(jnp.float32))
    row_dot = lax.optimization_barrier(jnp.sum(grad_ctx32 * context3.astype(jnp.float32), axis=2)).T[:, :, None]
    grad_scores = (probs32 * (grad_probs - row_dot)).astype(jnp.bfloat16).astype(jnp.float32)
    grad_q = (jnp.einsum('hqk,khd->qhd', grad_scores, keys.astype(jnp.float32)) * scale).astype(jnp.bfloat16)
    grad_k = (jnp.einsum('hqk,qhd->khd', grad_scores, queries.astype(jnp.float32)) * scale).astype(jnp.bfloat16)
    grad_v = jnp.einsum('hqk,qhd->khd', probs.astype(jnp.float32), grad_ctx32).astype(jnp.bfloat16)
    first = 0.9 * first_in.astype(jnp.float32) + 0.1 * grad_w
    second = 0.95 * second_in.astype(jnp.float32) + 0.05 * grad_w * grad_w
    step = first / (1.0 - 0.9 ** 10) / (jnp.sqrt(second / (1.0 - 0.95 ** 10)) + 1e-08)
    new_weight = (weight.astype(jnp.float32) - 0.001 * step).astype(jnp.bfloat16)
    return (hidden, grad_q.reshape(TOKENS, WIDTH_HEADS), grad_k.reshape(TOKENS, WIDTH_HEADS), grad_v.reshape(TOKENS, WIDTH_HEADS), new_weight, first.astype(jnp.bfloat16), second.astype(jnp.bfloat16))

def reference(query, key, value, resid, w_out, gain, grad_norm, grad_resid, moment_one, moment_two, delta, global_w, momentum):

    def one(index):
        rows = lambda a: lax.dynamic_slice_in_dim(a, index * TOKENS, TOKENS, 0)
        return replica_step(rows(query), rows(key), rows(value), rows(resid), w_out[index], gain[index], rows(grad_norm), rows(grad_resid), moment_one[index], moment_two[index])
    hidden, grad_q, grad_k, grad_v, new_w, first, second = lax.map(one, jnp.arange(N_ISLAND, dtype=jnp.int32))
    hidden = hidden.reshape(ALL_TOK, D)
    grad_q = grad_q.reshape(ALL_TOK, WIDTH_HEADS)
    grad_k = grad_k.reshape(ALL_TOK, WIDTH_HEADS)
    grad_v = grad_v.reshape(ALL_TOK, WIDTH_HEADS)
    average = lax.optimization_barrier(jnp.sum(delta.astype(jnp.float32), axis=0)) / N_ISLAND
    new_momentum = 0.9 * momentum + average
    new_global = global_w - 0.7 * (average + 0.9 * new_momentum)
    return (hidden, grad_q, grad_k, grad_v, new_w, first, second, new_global, new_momentum, new_global.astype(jnp.bfloat16))
```

```python
import functools

import jax
import jax.numpy as jnp
from jax import lax
from jax.experimental import pallas as pl
from jax.experimental.pallas import tpu as pltpu
from jax.sharding import PartitionSpec as P

HEAD = 128
SCALE = HEAD ** (-0.5)
MESH = pl.DeviceIdType.MESH
F32 = jnp.float32
BF16 = jnp.bfloat16
NZ = 8
NY = 4
Q = 1024
R = 32


def f32(a):
    return a.astype(F32)


def dot(a, b):
    return lax.dot_general(a, b, (((1,), (0,)), ((), ())), preferred_element_type=F32)


def dot_nt(a, b):
    return lax.dot_general(a, b, (((1,), (1,)), ((), ())), preferred_element_type=F32)


def dot_tn(a, b):
    return lax.dot_general(a, b, (((0,), (0,)), ((), ())), preferred_element_type=F32)


def kernel(
    q_in, k_in, v_in, resid_in, w_in, gain_ref, gn_in, gr_in, m1_in, m2_in, d_in, gl_in, mo_in,
    hid_out, dq_out, dk_out, dv_out, nw_out, nm1_out, nm2_out, ng_out, nmo_out, par_out,
    q4, kv, vv, w2, wp, res, gnv, grv, m1v, m2v, glv, mov,
    qs, prs, ctx, part, xrecv, rbuf, zbuf, xbuf, fin, hidv, gq, G,
    gco, gcs, gcr, gwacc, gws, gwr, dkacc, dvacc, dqv, dkv, dvv,
    yrecv, hbuf, xlrecv, pbuf, ngv, nmov,
    ld, od, ctx_s, ctx_r, w_s, w_r, xe_s, xe_r, ring_s, ring_r, fin_s, fin_r,
    a0_s, a0_r, ag_s, ag_r, xf_s, xf_r, gc_s, gc_r, gw_s, gw_r,
    ia_s, ia_r, ib_s, ib_r, ic_s, ic_r, id_s, id_r,
):
    isl = lax.axis_index("island")
    tp = lax.axis_index("tp")
    y, xl = isl // 2, lax.rem(isl, 2)
    xh, z, c = tp // 16, lax.rem(tp // 2, NZ), lax.rem(tp, 2)
    oc, oh = 1 - c, 1 - xh

    def tp_dev(a, b, d):
        return (isl, a * 16 + b * 2 + d)

    sib = tp_dev(xh, z, oc)
    opp = tp_dev(oh, z, c)
    opx = tp_dev(oh, z, oc)
    up = tp_dev(xh, lax.rem(z + 1, NZ), c)
    down = tp_dev(xh, lax.rem(z + NZ - 1, NZ), c)
    nxt = (up, down)
    ypeer = [(lax.rem(y + o, NY) * 2 + xl, tp) for o in (1, 2, 3)]
    xlpeer = (y * 2 + 1 - xl, tp)

    def rc(src, dst, ss, rs, dev):
        return pltpu.make_async_remote_copy(
            src_ref=src, dst_ref=dst, send_sem=ss, recv_sem=rs, device_id=dev, device_id_type=MESH
        )

    def cols(ref, at, width):
        return ref.at[:, pl.ds(pl.multiple_of(at * width, width), width)]

    loads = {}

    def load(name, src, dst):
        cp = pltpu.make_async_copy(src, dst, ld.at[len(loads)])
        loads[name] = cp
        cp.start()

    load("q", q_in, q4)
    load("k", k_in, kv)
    load("v", v_in, vv)
    load("wp", cols(w_in, c, 2048), wp.at[0])

    barrier = pltpu.get_barrier_semaphore()
    partners = [sib, opp, opx, up, down, xlpeer] + ypeer
    for dev in partners:
        pl.semaphore_signal(barrier, inc=1, device_id=dev, device_id_type=MESH)
    pl.semaphore_wait(barrier, len(partners))

    w_copy = rc(cols(w_in, oc, 2048), wp.at[1], w_s, w_r, sib)
    w_copy.start()

    a_copies = []
    for o in range(3):
        ny = lax.rem(y + o + 1, NY)
        for e in range(2):
            cp = rc(cols(d_in, ny * 2 + e, 512), yrecv.at[y, e], ia_s.at[o, e], ia_r.at[o, e], ypeer[o])
            cp.start()
            a_copies.append(cp)
    for e in range(2):
        load(f"d{e}", cols(d_in, y * 2 + e, 512), yrecv.at[y, e])
    for e in range(2):
        load(f"res{e}", resid_in.at[:, e * 2048 : (e + 1) * 2048], res.at[e])
        load(f"gn{e}", gn_in.at[:, e * 2048 : (e + 1) * 2048], gnv.at[e])
        load(f"gr{e}", gr_in.at[:, e * 2048 : (e + 1) * 2048], grv.at[e])
    load("gl", gl_in, glv)
    load("mo", mo_in, mov)
    for e in range(2):
        load(f"w{e}", w_in.at[:, e * 2048 : (e + 1) * 2048], w2.at[e])
        load(f"m1{e}", m1_in.at[:, e * 2048 : (e + 1) * 2048], m1v.at[e])
        load(f"m2{e}", m2_in.at[:, e * 2048 : (e + 1) * 2048], m2v.at[e])

    def places(g):
        return lax.rem(z - g + NZ, NZ), lax.rem(z + g, NZ)

    def ctx_copy(g):
        return rc(ctx.at[g, 0], ctx.at[g, 1], ctx_s.at[g], ctx_r.at[g], sib)

    def xe_copy(g):
        return rc(part.at[g, 1, oh], xrecv.at[g], xe_s.at[g], xe_r.at[g], opp)

    def attend(g):
        s0, s1 = places(g)
        qu = jnp.concatenate([q4[0, s0, 0], q4[0, s1, 1], q4[1, s0, 0], q4[1, s1, 1]], axis=0)
        qs[g] = qu
        scores = dot_nt(qu, kv[...]) * SCALE
        row = lax.broadcasted_iota(jnp.int32, (4 * R, 1), 0)
        odd = lax.rem(row // R, 2)
        qpos = (row // (2 * R)) * 512 + odd * R + lax.rem(row, R) + 64 * (s0 + odd * (s1 - s0))
        kpos = lax.broadcasted_iota(jnp.int32, (4 * R, 1024), 1)
        scores = jnp.where(kpos <= qpos, scores, -1e30)
        expo = jnp.exp(scores - jnp.max(scores, axis=1, keepdims=True))
        probs = (expo * (1.0 / jnp.sum(expo, axis=1, keepdims=True))).astype(BF16)
        prs[g] = probs
        ctx[g, 0] = dot(probs, vv[...]).astype(BF16)
        ctx_copy(g).start()

    def both(g):
        return jnp.concatenate([ctx[g, 0], ctx[g, 1]], axis=1)

    def project(g):
        ctx_copy(g).wait_recv()
        cx = both(g)
        for t in (1, 0):
            wt = wp[:, :, t * Q : (t + 1) * Q].reshape(256, Q)
            part[g, t] = dot(cx, wt).astype(BF16).reshape(2, 2, R, Q)
            if t == 1:
                xe_copy(g).start()

    def ring_copy(k, p, j):
        src = part.at[k + 1, 0, j, p] if j < 2 else part.at[k + 1, 1, xh, p]
        return rc(src, rbuf.at[k, p, j], ring_s.at[k, p, j], ring_r.at[k, p, j], nxt[p])

    def z_step(k, first=False):
        for h in range(2):
            for p in range(2):
                if not first:
                    ring_copy(k - 1, p, h).wait_recv()
                    part[k + 1, 0, h, p] = (
                        f32(part[k + 1, 0, h, p]) + f32(rbuf[k - 1, p, h])
                    ).astype(BF16)
                ring_copy(k, p, h).start()

    def x_step(k, first=False):
        xe_copy(k + 1).wait_recv()
        for p in range(2):
            total = f32(part[k + 1, 1, xh, p]) + f32(xrecv[k + 1, p])
            if not first:
                ring_copy(k - 1, p, 2).wait_recv()
                total = total + f32(rbuf[k - 1, p, 2])
            part[k + 1, 1, xh, p] = total.astype(BF16)
            ring_copy(k, p, 2).start()

    ib_copy = rc(hbuf, xlrecv, ib_s, ib_r, xlpeer)
    ic_copy = rc(pbuf.at[y, xl], pbuf.at[y, xl], ic_s, ic_r, xlpeer)
    id_copies = [rc(pbuf.at[y], pbuf.at[y], id_s.at[o], id_r.at[o], ypeer[o]) for o in range(3)]

    def over_y(e):
        return f32(yrecv[0, e]) + f32(yrecv[1, e]) + f32(yrecv[2, e]) + f32(yrecv[3, e])

    def outer_b():
        for cp in a_copies:
            cp.wait_recv()
        loads["d0"].wait()
        loads["d1"].wait()
        hbuf[...] = over_y(1 - xl).astype(BF16)
        ib_copy.start()

    def outer_c():
        ib_copy.wait_recv()
        loads["gl"].wait()
        loads["mo"].wait()
        average = (over_y(xl) + f32(xlrecv[...])) * 0.125
        moment = 0.9 * mov[...] + average
        new = glv[...] - 0.7 * (average + 0.9 * moment)
        nmov[...] = moment
        ngv[...] = new
        pbuf[y, xl] = new.astype(BF16)
        ic_copy.start()

    def outer_d():
        ic_copy.wait_recv()
        for cp in id_copies:
            cp.start()

    loads["q"].wait()
    loads["k"].wait()
    loads["v"].wait()
    attend(1)
    attend(2)
    loads["wp"].wait()
    w_copy.wait_recv()
    project(1)
    z_step(0, first=True)
    attend(3)
    project(2)
    project(3)
    x_step(0, first=True)

    def forward(k, carry):
        z_step(k)
        x_step(k)

        @pl.when(k <= 5)
        def _():
            g = lax.rem(k + 3, NZ)
            attend(g)
            project(g)

        @pl.when(k == 3)
        def _():
            outer_b()

        @pl.when(k == 5)
        def _():
            outer_c()

        return carry

    lax.fori_loop(1, 7, forward, 0)

    fin_copies = [
        rc(zbuf.at[xh, oc], fin.at[0], fin_s.at[0], fin_r.at[0], sib),
        rc(zbuf.at[oh, c], fin.at[1], fin_s.at[1], fin_r.at[1], opp),
        rc(zbuf.at[oh, oc], fin.at[2], fin_s.at[2], fin_r.at[2], opx),
        rc(xbuf.at[oc], fin.at[3], fin_s.at[3], fin_r.at[3], sib),
    ]
    for h in range(2):
        for p in range(2):
            ring_copy(6, p, h).wait_recv()
            zbuf[h, p] = (f32(part[0, 0, h, p]) + f32(rbuf[6, p, h])).astype(BF16)
    for i in (1, 2, 0):
        fin_copies[i].start()
    xe_copy(0).wait_recv()
    for p in range(2):
        ring_copy(6, p, 2).wait_recv()
        xbuf[p] = (f32(part[0, 1, xh, p]) + f32(xrecv[0, p]) + f32(rbuf[6, p, 2])).astype(BF16)
    fin_copies[3].start()
    for e in range(2):
        for name in ("res", "gn", "gr"):
            loads[f"{name}{e}"].wait()
    fin_copies[0].wait_recv()
    fin_copies[3].wait_recv()
    fin_copies[1].wait_recv()
    fin_copies[2].wait_recv()

    def of_block(cc, t):
        if t == 0:
            if cc is c:
                return f32(zbuf[xh, c]) + f32(fin[1])
            return f32(fin[0]) + f32(fin[2])
        return f32(xbuf[c]) if cc is c else f32(fin[3])

    blocks = [(cc, t) for cc in (c, oc) for t in range(2)]
    gain_low, gain_high = gain_ref[:, :2048], gain_ref[:, 2048:]
    low = c == 0
    values, scaleds = [], []
    square = jnp.zeros((R, 1), F32)
    cross = jnp.zeros((R, 1), F32)
    for cc, t in blocks:
        at = slice(t * Q, (t + 1) * Q)
        hid = (f32(res[cc, :, at]) + of_block(cc, t)).astype(BF16)
        hidv[cc, :, at] = hid
        val = f32(hid)
        first_half = low if cc is c else jnp.logical_not(low)
        gain = jnp.where(first_half, f32(gain_low[:, at]), f32(gain_high[:, at]))
        scaled = f32(gnv[cc, :, at]) * gain
        square = square + jnp.sum(val * val, axis=1, keepdims=True)
        cross = cross + jnp.sum(scaled * val, axis=1, keepdims=True)
        values.append(val)
        scaleds.append(scaled)
    rstd = lax.rsqrt(square * (1.0 / 4096) + 1e-05)
    inner = cross * rstd * (1.0 / 4096)
    for (cc, t), val, scaled in zip(blocks, values, scaleds):
        at = slice(t * Q, (t + 1) * Q)
        back = f32(grv[cc, :, at]) + rstd * (scaled - val * rstd * inner)
        gq[cc, t] = back.astype(BF16)
    a0_copies = [
        rc(gq.at[c, 0], G.at[0, 0, xh, c], a0_s.at[2], a0_r.at[2], opp),
        rc(gq.at[oc, 0], G.at[0, 0, xh, c], a0_s.at[3], a0_r.at[3], opx),
        rc(gq.at[oc, 0], G.at[0, 0, xh, c], a0_s.at[0], a0_r.at[0], sib),
        rc(gq.at[oc, 1], G.at[0, 1, xh, c], a0_s.at[1], a0_r.at[1], sib),
    ]
    for cp in a0_copies:
        cp.start()
    for t in range(2):
        G[0, t, xh, c] = gq[c, t]
    gwacc[...] = jnp.zeros_like(gwacc)
    dkacc[...] = jnp.zeros_like(dkacc)
    dvacc[...] = jnp.zeros_like(dvacc)

    outs = []

    def emit(src, dst):
        cp = pltpu.make_async_copy(src, dst, od.at[len(outs)])
        outs.append(cp)
        cp.start()

    for e in range(2):
        emit(hidv.at[e], hid_out.at[:, e * 2048 : (e + 1) * 2048])
    emit(ngv, ng_out)
    emit(nmov, nmo_out)

    def ag_copy(k, p, j):
        t, h = (0, j) if j < 2 else (1, xh)
        return rc(
            G.at[k, t, h, p], G.at[k + 1, t, h, p], ag_s.at[k, p, j], ag_r.at[k, p, j], nxt[p]
        )

    def xf_copy(g, p):
        return rc(G.at[g, 1, xh, p], G.at[g, 1, xh, p], xf_s.at[g, p], xf_r.at[g, p], opp)

    for cp in (a0_copies[2], a0_copies[3], a0_copies[0], a0_copies[1]):
        cp.wait_recv()
    for j in (2, 0, 1):
        for p in range(2):
            ag_copy(0, p, j).start()
            if j == 2:
                xf_copy(0, p).start()

    def weigh(g):
        for p in range(2):
            xf_copy(g, p).wait_recv()
        gc = None
        cx = both(g)
        for t in range(2):
            gt = G[g, t].reshape(4 * R, Q)
            wt = wp[:, :, t * Q : (t + 1) * Q].reshape(256, Q)
            piece = dot_nt(gt, wt)
            gc = piece if gc is None else gc + piece
        gco[g] = gc[:, :HEAD]
        gcs[g] = gc[:, HEAD:]
        gc_copy(g).start()
        for t in range(2):
            gt = G[g, t].reshape(4 * R, Q)
            gwacc[:, t * Q : (t + 1) * Q] += dot_tn(cx, gt)

    def gc_copy(g):
        return rc(gcs.at[g], gcr.at[g], gc_s.at[g], gc_r.at[g], sib)

    def attend_back(g):
        gc_copy(g).wait_recv()
        s0, s1 = places(g)
        gc = (gco[g] + gcr[g]).astype(BF16)
        probs = prs[g]
        row_dot = jnp.sum(f32(gc) * f32(ctx[g, 0]), axis=1, keepdims=True)
        gs = (f32(probs) * (dot_nt(gc, vv[...]) - row_dot)).astype(BF16)
        dq = (dot(gs, kv[...]) * SCALE).astype(BF16)
        for h in range(2):
            for p, s in enumerate((s0, s1)):
                dqv[h, s, p] = dq[(2 * h + p) * R : (2 * h + p + 1) * R]
        dkacc[...] += dot_tn(gs, qs[g])
        dvacc[...] += dot_tn(probs, gc)

    def backward(k, carry):
        for j in (2, 0, 1):
            for p in range(2):
                ag_copy(k, p, j).wait_recv()

                @pl.when(k < 6)
                def _():
                    ag_copy(k + 1, p, j).start()

                if j == 2:
                    xf_copy(k + 1, p).start()

        weigh(k)

        @pl.when(k >= 1)
        def _():
            attend_back(k - 1)

        @pl.when(k == 1)
        def _():
            outer_d()

        return carry

    lax.fori_loop(0, 7, backward, 0)

    weigh(7)
    gws[...] = gwacc[HEAD:].astype(BF16)
    gw_copy = rc(gws, gwr, gw_s, gw_r, sib)
    gw_copy.start()
    attend_back(6)
    attend_back(7)
    dkv[...] = (dkacc[...] * SCALE).astype(BF16)
    dvv[...] = dvacc[...].astype(BF16)
    emit(dqv, dq_out)
    emit(dkv, dk_out)
    emit(dvv, dv_out)
    for cp in id_copies:
        cp.wait_recv()
    for i in range(8):
        emit(pbuf.at[i // 2, i % 2], par_out.at[:, i * 512 : (i + 1) * 512])

    for e in range(2):
        for name in ("w", "m1", "m2"):
            loads[f"{name}{e}"].wait()

    def adam(cc, grad_of):
        for i in range(8):
            rows = slice(i * 16, (i + 1) * 16)
            grad = grad_of(rows)
            first = 0.9 * f32(m1v[cc, rows]) + 0.1 * grad
            second = 0.95 * f32(m2v[cc, rows]) + 0.05 * grad * grad
            update = (first * (1.0 / (1.0 - 0.9**10))) / (
                jnp.sqrt(second * (1.0 / (1.0 - 0.95**10))) + 1e-08
            )
            w2[cc, rows] = (f32(w2[cc, rows]) - 0.001 * update).astype(BF16)
            m1v[cc, rows] = first.astype(BF16)
            m2v[cc, rows] = second.astype(BF16)
        for src, dst in ((w2, nw_out), (m1v, nm1_out), (m2v, nm2_out)):
            emit(src.at[cc], cols(dst, cc, 2048))

    adam(c, lambda rows: gwacc[rows])
    gw_copy.wait_recv()
    adam(oc, lambda rows: f32(gwr[rows]))

    w_copy.wait_send()
    gw_copy.wait_send()
    for cp in a_copies + fin_copies + a0_copies + id_copies + [ib_copy, ic_copy]:
        cp.wait_send()

    def drain8(g, carry):
        ctx_copy(g).wait_send()
        xe_copy(g).wait_send()
        gc_copy(g).wait_send()
        for p in range(2):
            xf_copy(g, p).wait_send()
        return carry

    lax.fori_loop(0, 8, drain8, 0)

    def drain7(k, carry):
        for p in range(2):
            for j in range(3):
                ring_copy(k, p, j).wait_send()
                ag_copy(k, p, j).wait_send()
        return carry

    lax.fori_loop(0, 7, drain7, 0)
    for cp in outs:
        cp.wait()


def per_device(
    query, key, value, resid, w_out, gain, grad_norm, grad_resid, moment_one, moment_two,
    delta, global_w, momentum,
):
    any_spec = pl.BlockSpec(memory_space=pl.ANY)
    dma = pltpu.SemaphoreType.DMA

    def vm(shape, dtype=BF16):
        return pltpu.VMEM(shape, dtype)

    def shape(dims, dtype=BF16):
        return jax.ShapeDtypeStruct(dims, dtype)

    scratch = [
        vm((2, 8, 2, R, HEAD)), vm((1024, HEAD)), vm((1024, HEAD)), vm((2, 128, 2048)),
        vm((2, 128, 2048)), vm((2, R, 2048)), vm((2, R, 2048)), vm((2, R, 2048)),
        vm((2, 128, 2048)), vm((2, 128, 2048)), vm((128, 512), F32), vm((128, 512), F32),
        vm((8, 128, HEAD)), vm((8, 128, 1024)), vm((8, 2, 128, HEAD)),
        vm((8, 2, 2, 2, R, Q)), vm((8, 2, R, Q)), vm((7, 2, 3, R, Q)),
        vm((2, 2, R, Q)), vm((2, R, Q)), vm((4, R, Q)),
        vm((2, R, 2048)), vm((2, 2, R, Q)), vm((8, 2, 2, 2, R, Q)),
        vm((8, 128, HEAD), F32), vm((8, 128, HEAD), F32), vm((8, 128, HEAD), F32),
        vm((256, 2048), F32), vm((128, 2048)), vm((128, 2048)),
        vm((1024, HEAD), F32), vm((1024, HEAD), F32),
        vm((2, 8, 2, R, HEAD)), vm((1024, HEAD)), vm((1024, HEAD)),
        vm((4, 2, 128, 512)), vm((128, 512)), vm((128, 512)), vm((4, 2, 128, 512)),
        vm((128, 512), F32), vm((128, 512), F32),
        dma((20,)), dma((24,)), dma((8,)), dma((8,)), dma, dma,
        dma((8,)), dma((8,)), dma((7, 2, 3)), dma((7, 2, 3)),
        dma((4,)), dma((4,)), dma((4,)), dma((4,)),
        dma((7, 2, 3)), dma((7, 2, 3)), dma((8, 2)), dma((8, 2)),
        dma((8,)), dma((8,)), dma, dma,
        dma((3, 2)), dma((3, 2)), dma, dma, dma, dma, dma((3,)), dma((3,)),
    ]
    hidden, dq, dk, dv, nw, nm1, nm2, ng, nmo, par = pl.pallas_call(
        kernel,
        out_shape=[
            shape((R, 4096)), shape((2, 8, 2, R, HEAD)), shape((1024, HEAD)), shape((1024, HEAD)),
            shape((128, 4096)), shape((128, 4096)), shape((128, 4096)),
            shape((128, 512), F32), shape((128, 512), F32), shape((128, 4096)),
        ],
        in_specs=[any_spec] * 5 + [pl.BlockSpec(memory_space=pltpu.VMEM)] + [any_spec] * 7,
        out_specs=[any_spec] * 10,
        scratch_shapes=scratch,
        compiler_params=pltpu.CompilerParams(
            collective_id=0, has_side_effects=True, vmem_limit_bytes=58 << 20
        ),
        cost_estimate=pl.CostEstimate(flops=5 * 10**9, bytes_accessed=12 << 20, transcendentals=10**6),
        name="whole_step",
    )(
        query.reshape(2, 8, 2, R, HEAD), key, value, resid, w_out[0], gain, grad_norm, grad_resid,
        moment_one[0], moment_two[0], delta[0], global_w, momentum,
    )
    return (
        hidden, dq.reshape(1024, HEAD), dk, dv, nw[None], nm1[None], nm2[None], ng, nmo, par,
    )


def solution(mesh):
    return jax.shard_map(
        per_device,
        mesh=mesh,
        in_specs=(
            P("island", "tp"),
            P("island", "tp"),
            P("island", "tp"),
            P(("island", "tp"), None),
            P("island", "tp", None),
            P("island", None),
            P(("island", "tp"), None),
            P(("island", "tp"), None),
            P("island", "tp", None),
            P("island", "tp", None),
            P("island", "tp", None),
            P("tp", "island"),
            P("tp", "island"),
        ),
        out_specs=(
            P(("island", "tp"), None),
            P("island", "tp"),
            P("island", "tp"),
            P("island", "tp"),
            P("island", "tp", None),
            P("island", "tp", None),
            P("island", "tp", None),
            P("tp", "island"),
            P("tp", "island"),
            P("tp", None),
        ),
        check_vma=False,
    )
```

```python
import functools

import jax
import jax.numpy as jnp
from jax import lax
from jax.experimental import pallas as pl
from jax.experimental.pallas import tpu as pltpu
from jax.sharding import PartitionSpec as P

HEAD = 128
SCALE = HEAD ** (-0.5)
MESH = pl.DeviceIdType.MESH
F32 = jnp.float32
BF16 = jnp.bfloat16
NZ = 8
NY = 4
QZ = 896
QX = 2048 - QZ
SPAN = (slice(0, QZ), slice(QZ, 2048))
R = 32


def f32(a):
    return a.astype(F32)


def dot(a, b):
    return lax.dot_general(a, b, (((1,), (0,)), ((), ())), preferred_element_type=F32)


def dot_nt(a, b):
    return lax.dot_general(a, b, (((1,), (1,)), ((), ())), preferred_element_type=F32)


def dot_tn(a, b):
    return lax.dot_general(a, b, (((0,), (0,)), ((), ())), preferred_element_type=F32)


def kernel(
    q_in, k_in, v_in, resid_in, w_in, gain_ref, gn_in, gr_in, d_in, gl_in, mo_in,
    hid_out, dq_out, dk_out, dv_out, ng_out, nmo_out, par_out, gw_out,
    q4, kv, vv, wp, res, gnv, grv, glv, mov,
    qs, prs, ctx, part0, part1, xrecv, rbuf0, rbuf1, zbuf, xbuf, fin0, fin1, gq0, gq1, G0, G1,
    gco, gcs, gcr, gwacc, gws, gwo, dkacc, dvacc, yrecv, hbuf, xlrecv,
    hidv, dqv, dkv, dvv, ngv, nmov, pbuf,
    ld, od, ctx_s, ctx_r, w_s, w_r, xe_s, xe_r, ring_s, ring_r, fin_s, fin_r,
    a0_s, a0_r, ag_s, ag_r, xf_s, xf_r, gc_s, gc_r, gw_s, gw_r,
    ia_s, ia_r, ib_s, ib_r, ic_s, ic_r, id_s, id_r,
):
    isl = lax.axis_index("island")
    tp = lax.axis_index("tp")
    y, xl = isl // 2, lax.rem(isl, 2)
    xh, z, c = tp // 16, lax.rem(tp // 2, NZ), lax.rem(tp, 2)
    oc, oh = 1 - c, 1 - xh

    def tp_dev(a, b, d):
        return (isl, a * 16 + b * 2 + d)

    sib = tp_dev(xh, z, oc)
    opp = tp_dev(oh, z, c)
    opx = tp_dev(oh, z, oc)
    up = tp_dev(xh, lax.rem(z + 1, NZ), c)
    down = tp_dev(xh, lax.rem(z + NZ - 1, NZ), c)
    nxt = (up, down)
    ypeer = [(lax.rem(y + o, NY) * 2 + xl, tp) for o in (1, 2, 3)]
    xlpeer = (y * 2 + 1 - xl, tp)

    def rc(src, dst, ss, rs, dev):
        return pltpu.make_async_remote_copy(
            src_ref=src, dst_ref=dst, send_sem=ss, recv_sem=rs, device_id=dev, device_id_type=MESH
        )

    def cols(ref, at, width):
        return ref.at[:, pl.ds(pl.multiple_of(at * width, width), width)]

    loads = {}

    def load(name, src, dst):
        cp = pltpu.make_async_copy(src, dst, ld.at[len(loads)])
        loads[name] = cp
        cp.start()

    load("q", q_in, q4)
    load("k", k_in, kv)
    load("v", v_in, vv)
    load("wp", cols(w_in, c, 2048), wp.at[0])

    barrier = pltpu.get_barrier_semaphore()
    partners = [sib, opp, opx, up, down, xlpeer] + ypeer
    for dev in partners:
        pl.semaphore_signal(barrier, inc=1, device_id=dev, device_id_type=MESH)

    def places(g):
        return lax.rem(z - g + NZ, NZ), lax.rem(z + g, NZ)

    def ctx_copy(g):
        return rc(ctx.at[g, 0], ctx.at[g, 1], ctx_s.at[g], ctx_r.at[g], sib)

    def xe_copy(g):
        return rc(part1.at[g, oh], xrecv.at[g], xe_s.at[g], xe_r.at[g], opp)

    def attend(g):
        s0, s1 = places(g)
        qu = jnp.concatenate([q4[0, s0, 0], q4[0, s1, 1], q4[1, s0, 0], q4[1, s1, 1]], axis=0)
        qs[g] = qu
        scores = dot_nt(qu, kv[...]) * SCALE
        row = lax.broadcasted_iota(jnp.int32, (4 * R, 1), 0)
        odd = lax.rem(row // R, 2)
        qpos = (row // (2 * R)) * 512 + odd * R + lax.rem(row, R) + 64 * (s0 + odd * (s1 - s0))
        kpos = lax.broadcasted_iota(jnp.int32, (4 * R, 1024), 1)
        scores = jnp.where(kpos <= qpos, scores, -1e30)
        expo = jnp.exp(scores - jnp.max(scores, axis=1, keepdims=True))
        probs = (expo * (1.0 / jnp.sum(expo, axis=1, keepdims=True))).astype(BF16)
        prs[g] = probs
        ctx[g, 0] = dot(probs, vv[...]).astype(BF16)

    def both(g):
        return jnp.concatenate([ctx[g, 0], ctx[g, 1]], axis=1)

    def project(g, order=(1, 0)):
        ctx_copy(g).wait_recv()
        cx = both(g)
        for t in order:
            wt = wp[:, :, SPAN[t]].reshape(256, -1)
            out = dot(cx, wt).astype(BF16).reshape(2, 2, R, -1)
            if t == 1:
                part1[g] = out
                xe_copy(g).start()
            else:
                part0[g] = out

    halves = (oh, xh, xh)

    def ring_copy(k, p, j):
        if j < 2:
            src, dst = part0.at[k + 1, halves[j], p], rbuf0.at[k, p, j]
        else:
            src, dst = part1.at[k + 1, xh, p], rbuf1.at[k, p]
        return rc(src, dst, ring_s.at[k, p, j], ring_r.at[k, p, j], nxt[p])

    def z_step(k, first=False):
        for j in range(2):
            h = halves[j]
            for p in range(2):
                if not first:
                    ring_copy(k - 1, p, j).wait_recv()
                    part0[k + 1, h, p] = (f32(part0[k + 1, h, p]) + f32(rbuf0[k - 1, p, j])).astype(BF16)
                ring_copy(k, p, j).start()

    def x_step(k, first=False):
        xe_copy(k + 1).wait_recv()
        for p in range(2):
            total = f32(part1[k + 1, xh, p]) + f32(xrecv[k + 1, p])
            if not first:
                ring_copy(k - 1, p, 2).wait_recv()
                total = total + f32(rbuf1[k - 1, p])
            part1[k + 1, xh, p] = total.astype(BF16)
            ring_copy(k, p, 2).start()

    ib_copy = rc(hbuf, xlrecv, ib_s, ib_r, xlpeer)
    ic_copy = rc(pbuf.at[y, xl], pbuf.at[y, xl], ic_s, ic_r, xlpeer)
    id_copies = [rc(pbuf.at[y], pbuf.at[y], id_s.at[o], id_r.at[o], ypeer[o]) for o in range(3)]

    def over_y(e):
        return f32(yrecv[0, e]) + f32(yrecv[1, e]) + f32(yrecv[2, e]) + f32(yrecv[3, e])

    def outer_b():
        for cp in a_copies:
            cp.wait_recv()
        loads["d0"].wait()
        loads["d1"].wait()
        hbuf[...] = over_y(1 - xl).astype(BF16)
        ib_copy.start()

    def outer_c():
        ib_copy.wait_recv()
        loads["gl"].wait()
        loads["mo"].wait()
        average = (over_y(xl) + f32(xlrecv[...])) * 0.125
        moment = 0.9 * mov[...] + average
        new = glv[...] - 0.7 * (average + 0.9 * moment)
        nmov[...] = moment
        ngv[...] = new
        pbuf[y, xl] = new.astype(BF16)
        ic_copy.start()

    def outer_d():
        ic_copy.wait_recv()
        for cp in id_copies:
            cp.start()

    loads["q"].wait()
    loads["k"].wait()
    loads["v"].wait()
    attend(1)
    pl.semaphore_wait(barrier, len(partners))
    w_copy = rc(cols(w_in, oc, 2048), wp.at[1], w_s, w_r, sib)
    w_copy.start()
    ctx_copy(1).start()
    a_copies = []
    for o in range(3):
        ny = lax.rem(y + o + 1, NY)
        for e in range(2):
            cp = rc(cols(d_in, ny * 2 + e, 512), yrecv.at[y, e], ia_s.at[o, e], ia_r.at[o, e], ypeer[o])
            cp.start()
            a_copies.append(cp)
    for e in range(2):
        load(f"d{e}", cols(d_in, y * 2 + e, 512), yrecv.at[y, e])
    for e in range(2):
        load(f"res{e}", resid_in.at[:, e * 2048 : (e + 1) * 2048], res.at[e])
        load(f"gn{e}", gn_in.at[:, e * 2048 : (e + 1) * 2048], gnv.at[e])
        load(f"gr{e}", gr_in.at[:, e * 2048 : (e + 1) * 2048], grv.at[e])
    load("gl", gl_in, glv)
    load("mo", mo_in, mov)
    attend(2)
    ctx_copy(2).start()
    loads["wp"].wait()
    w_copy.wait_recv()
    project(1, order=(0, 1))
    z_step(0, first=True)
    attend(3)
    ctx_copy(3).start()
    project(2)
    project(3)

    def forward_step(k, second=False):
        g = lax.rem(k + 3, NZ)
        z_step(k)
        attend(g)
        ctx_copy(g).start()
        x_step(k - 1, first=second)
        project(g)

    forward_step(1, second=True)

    def forward(k, carry):
        forward_step(k)

        @pl.when(k == 3)
        def _():
            outer_b()

        @pl.when(k == 5)
        def _():
            outer_c()

        return carry

    lax.fori_loop(2, 6, forward, 0)
    z_step(6)
    x_step(5)

    fin_copies = [
        rc(zbuf.at[xh, oc], fin0.at[0], fin_s.at[0], fin_r.at[0], sib),
        rc(zbuf.at[oh, c], fin0.at[1], fin_s.at[1], fin_r.at[1], opp),
        rc(zbuf.at[oh, oc], fin0.at[2], fin_s.at[2], fin_r.at[2], opx),
        rc(xbuf.at[oc], fin1, fin_s.at[3], fin_r.at[3], sib),
    ]

    def z_last(j):
        for p in range(2):
            ring_copy(6, p, j).wait_recv()
            zbuf[halves[j], p] = (f32(part0[0, halves[j], p]) + f32(rbuf0[6, p, j])).astype(BF16)

    z_last(0)
    fin_copies[1].start()
    fin_copies[2].start()
    x_step(6)
    z_last(1)
    fin_copies[0].start()
    xe_copy(0).wait_recv()
    for p in range(2):
        ring_copy(6, p, 2).wait_recv()
        xbuf[p] = (f32(part1[0, xh, p]) + f32(xrecv[0, p]) + f32(rbuf1[6, p])).astype(BF16)
    fin_copies[3].start()
    for e in range(2):
        for name in ("res", "gn", "gr"):
            loads[f"{name}{e}"].wait()
    fin_copies[0].wait_recv()
    fin_copies[3].wait_recv()
    fin_copies[1].wait_recv()
    fin_copies[2].wait_recv()

    def of_block(cc, t):
        if t == 0:
            if cc is c:
                return f32(zbuf[xh, c]) + f32(fin0[1])
            return f32(fin0[0]) + f32(fin0[2])
        return f32(xbuf[c]) if cc is c else f32(fin1[...])

    blocks = [(oc, 1), (oc, 0), (c, 0), (c, 1)]
    low = c == 0
    values, scaleds = [], []
    square = jnp.zeros((R, 1), F32)
    cross = jnp.zeros((R, 1), F32)
    for cc, t in blocks:
        at = SPAN[t]
        hid = (f32(res[cc, :, at]) + of_block(cc, t)).astype(BF16)
        hidv[cc, :, at] = hid
        val = f32(hid)
        first_half = low if cc is c else jnp.logical_not(low)
        gain = jnp.where(
            first_half, f32(gain_ref[:, at]), f32(gain_ref[:, at.start + 2048 : at.stop + 2048])
        )
        scaled = f32(gnv[cc, :, at]) * gain
        square = square + jnp.sum(val * val, axis=1, keepdims=True)
        cross = cross + jnp.sum(scaled * val, axis=1, keepdims=True)
        values.append(val)
        scaleds.append(scaled)
    rstd = lax.rsqrt(square * (1.0 / 4096) + 1e-05)
    inner = cross * rstd * (1.0 / 4096)
    a0_copies = [
        rc(gq0.at[1], G0.at[0, xh, c], a0_s.at[0], a0_r.at[0], sib),
        rc(gq1, G1.at[0, xh, c], a0_s.at[1], a0_r.at[1], sib),
        rc(gq0.at[0], G0.at[0, xh, c], a0_s.at[2], a0_r.at[2], opp),
        rc(gq0.at[1], G0.at[0, xh, c], a0_s.at[3], a0_r.at[3], opx),
    ]
    for (cc, t), val, scaled in zip(blocks, values, scaleds):
        back = (f32(grv[cc, :, SPAN[t]]) + rstd * (scaled - val * rstd * inner)).astype(BF16)
        if t == 1 and cc is oc:
            gq1[...] = back
            a0_copies[1].start()
        elif t == 1:
            G1[0, xh, c] = back
        elif cc is oc:
            gq0[1] = back
            a0_copies[3].start()
            a0_copies[0].start()
        else:
            gq0[0] = back
            a0_copies[2].start()
            G0[0, xh, c] = back

    outs = []

    def emit(src, dst):
        cp = pltpu.make_async_copy(src, dst, od.at[len(outs)])
        outs.append(cp)
        cp.start()

    def ag_copy(k, p, j):
        if j == 2:
            src, dst = G1.at[k, xh, p], G1.at[k + 1, xh, p]
        else:
            h = (xh, oh)[j]
            src, dst = G0.at[k, h, p], G0.at[k + 1, h, p]
        return rc(src, dst, ag_s.at[k, p, j], ag_r.at[k, p, j], nxt[p])

    def xf_copy(g, p):
        return rc(G1.at[g, xh, p], G1.at[g, xh, p], xf_s.at[g, p], xf_r.at[g, p], opp)

    def lead(k, last=False):
        for p in range(2):
            ag_copy(k, p, 2).wait_recv()
            if not last:
                ag_copy(k + 1, p, 2).start()
            xf_copy(k + 1, p).start()

    a0_copies[1].wait_recv()
    for p in range(2):
        ag_copy(0, p, 2).start()
        xf_copy(0, p).start()
    a0_copies[0].wait_recv()
    for p in range(2):
        ag_copy(0, p, 0).start()
    gwacc[...] = jnp.zeros_like(gwacc)
    dkacc[...] = jnp.zeros_like(dkacc)
    dvacc[...] = jnp.zeros_like(dvacc)
    a0_copies[2].wait_recv()
    a0_copies[3].wait_recv()
    for p in range(2):
        ag_copy(0, p, 1).start()
    lead(0)
    for e in range(2):
        emit(hidv.at[e], hid_out.at[:, e * 2048 : (e + 1) * 2048])
    emit(ngv, ng_out)
    emit(nmov, nmo_out)

    def weigh(g, last=False):
        for p in range(2):
            xf_copy(g, p).wait_recv()
        cx = both(g)
        gc = None
        for t, G in enumerate((G0, G1)):
            piece = dot_nt(G[g].reshape(4 * R, -1), wp[:, :, SPAN[t]].reshape(256, -1))
            gc = piece if gc is None else gc + piece
        gco[g] = gc[:, :HEAD]
        gcs[g] = gc[:, HEAD:]
        gc_copy(g).start()
        for t, G in enumerate((G0, G1)):
            total = gwacc[:, SPAN[t]] + dot_tn(cx, G[g].reshape(4 * R, -1))
            if last:
                gws[:, SPAN[t]] = total[HEAD:].astype(BF16)
                gwo[:, SPAN[t]] = total[:HEAD].astype(BF16)
            else:
                gwacc[:, SPAN[t]] = total

    def gc_copy(g):
        return rc(gcs.at[g], gcr.at[g], gc_s.at[g], gc_r.at[g], sib)

    def attend_back(g):
        gc_copy(g).wait_recv()
        s0, s1 = places(g)
        gc = (gco[g] + gcr[g]).astype(BF16)
        probs = prs[g]
        row_dot = jnp.sum(f32(gc) * f32(ctx[g, 0]), axis=1, keepdims=True)
        gs = (f32(probs) * (dot_nt(gc, vv[...]) - row_dot)).astype(BF16)
        dq = (dot(gs, kv[...]) * SCALE).astype(BF16)
        for h in range(2):
            for p, s in enumerate((s0, s1)):
                dqv[h, s, p] = dq[(2 * h + p) * R : (2 * h + p + 1) * R]
        dkacc[...] += dot_tn(gs, qs[g])
        dvacc[...] += dot_tn(probs, gc)

    def follow(k):
        for j in range(2):
            for p in range(2):
                ag_copy(k, p, j).wait_recv()
                ag_copy(k + 1, p, j).start()

    def backward(k, carry):
        follow(k)

        @pl.when(k < 5)
        def _():
            lead(k + 1)

        @pl.when(k == 5)
        def _():
            lead(6, last=True)

        weigh(k)

        @pl.when(k >= 1)
        def _():
            attend_back(k - 1)

        @pl.when(k == 1)
        def _():
            outer_d()

        return carry

    lax.fori_loop(0, 6, backward, 0)
    weigh(6)
    attend_back(5)
    for cp in id_copies:
        cp.wait_recv()
    for i in range(8):
        emit(pbuf.at[i // 2, i % 2], par_out.at[:, i * 512 : (i + 1) * 512])
    attend_back(6)
    for j in range(2):
        for p in range(2):
            ag_copy(6, p, j).wait_recv()
    weigh(7, last=True)
    gw_copy = rc(gws, gw_out.at[c], gw_s, gw_r, sib)
    gw_copy.start()
    emit(gwo, gw_out.at[c])
    attend_back(7)
    emit(dqv, dq_out)
    dkv[...] = (dkacc[...] * SCALE).astype(BF16)
    emit(dkv, dk_out)
    dvv[...] = dvacc[...].astype(BF16)
    emit(dvv, dv_out)

    w_copy.wait_send()
    gw_copy.wait_send()
    for cp in a_copies + fin_copies + a0_copies + id_copies + [ib_copy, ic_copy]:
        cp.wait_send()

    def drain8(g, carry):
        ctx_copy(g).wait_send()
        xe_copy(g).wait_send()
        gc_copy(g).wait_send()
        for p in range(2):
            xf_copy(g, p).wait_send()
        return carry

    lax.fori_loop(0, 8, drain8, 0)

    def drain7(k, carry):
        for p in range(2):
            for j in range(3):
                ring_copy(k, p, j).wait_send()
                ag_copy(k, p, j).wait_send()
        return carry

    lax.fori_loop(0, 7, drain7, 0)
    gw_copy.wait_recv()
    for cp in outs:
        cp.wait()


def finish(
    hid_in, dq_in, dk_in, dv_in, ng_in, nmo_in, par_in, gw_in, w_in, m1_in, m2_in,
    hid_out, dq_out, dk_out, dv_out, nw_out, nm1_out, nm2_out, ng_out, nmo_out, par_out,
    gw, w, m1, m2, par, hid, dq, dk, dv, ng, nmo, ld, od,
):
    outs, loads = [], []

    def emit(src, dst):
        cp = pltpu.make_async_copy(src, dst, od.at[len(outs)])
        outs.append(cp)
        cp.start()

    def load(src, dst):
        cp = pltpu.make_async_copy(src, dst, ld.at[len(loads)])
        loads.append(cp)
        cp.start()

    for i in range(4):
        rows = slice(i * 32, (i + 1) * 32)
        for e in range(2):
            load(gw_in.at[e, rows], gw.at[e, rows])
        load(m1_in.at[rows], m1.at[rows])
        load(m2_in.at[rows], m2.at[rows])
        load(w_in.at[rows], w.at[rows])
    passed = (
        (hid_in, hid, hid_out), (dq_in, dq, dq_out), (dk_in, dk, dk_out), (dv_in, dv, dv_out),
        (ng_in, ng, ng_out), (nmo_in, nmo, nmo_out), (par_in, par, par_out),
    )
    for src, mid, _ in passed:
        load(src, mid)
    for i in range(4):
        for cp in loads[5 * i : 5 * i + 5]:
            cp.wait()
        for rows in (slice(i * 32, i * 32 + 16), slice(i * 32 + 16, i * 32 + 32)):
            for e in range(2):
                at = slice(e * 2048, (e + 1) * 2048)
                grad = f32(gw[e, rows])
                first = 0.9 * f32(m1[rows, at]) + 0.1 * grad
                second = 0.95 * f32(m2[rows, at]) + 0.05 * grad * grad
                update = (first * (1.0 / (1.0 - 0.9**10))) / (
                    jnp.sqrt(second * (1.0 / (1.0 - 0.95**10))) + 1e-08
                )
                w[rows, at] = (f32(w[rows, at]) - 0.001 * update).astype(BF16)
                m1[rows, at] = first.astype(BF16)
                m2[rows, at] = second.astype(BF16)
        rows = slice(i * 32, (i + 1) * 32)
        for src, dst in ((w, nw_out), (m1, nm1_out), (m2, nm2_out)):
            emit(src.at[rows], dst.at[rows])
        for at in (2 * i, 2 * i + 1):
            if at < len(passed):
                loads[20 + at].wait()
                emit(passed[at][1], passed[at][2])
    for cp in outs:
        cp.wait()


def per_device(
    query, key, value, resid, w_out, gain, grad_norm, grad_resid, moment_one, moment_two,
    delta, global_w, momentum,
):
    any_spec = pl.BlockSpec(memory_space=pl.ANY)
    dma = pltpu.SemaphoreType.DMA

    def vm(shape, dtype=BF16):
        return pltpu.VMEM(shape, dtype)

    def shape(dims, dtype=BF16):
        return jax.ShapeDtypeStruct(dims, dtype)

    scratch = [
        vm((2, 8, 2, R, HEAD)), vm((1024, HEAD)), vm((1024, HEAD)),
        vm((2, 128, 2048)), vm((2, R, 2048)), vm((2, R, 2048)), vm((2, R, 2048)),
        vm((128, 512), F32), vm((128, 512), F32),
        vm((8, 128, HEAD)), vm((8, 128, 1024)), vm((8, 2, 128, HEAD)),
        vm((8, 2, 2, R, QZ)), vm((8, 2, 2, R, QX)), vm((8, 2, R, QX)),
        vm((7, 2, 2, R, QZ)), vm((7, 2, R, QX)),
        vm((2, 2, R, QZ)), vm((2, R, QX)), vm((3, R, QZ)), vm((R, QX)),
        vm((2, R, QZ)), vm((R, QX)), vm((8, 2, 2, R, QZ)), vm((8, 2, 2, R, QX)),
        vm((8, 128, HEAD), F32), vm((8, 128, HEAD), F32), vm((8, 128, HEAD), F32),
        vm((256, 2048), F32), vm((128, 2048)), vm((128, 2048)),
        vm((1024, HEAD), F32), vm((1024, HEAD), F32),
        vm((4, 2, 128, 512)), vm((128, 512)), vm((128, 512)),
        vm((2, R, 2048)), vm((2, 8, 2, R, HEAD)), vm((1024, HEAD)), vm((1024, HEAD)),
        vm((128, 512), F32), vm((128, 512), F32), vm((4, 2, 128, 512)),
        dma((14,)), dma((16,)), dma((8,)), dma((8,)), dma, dma,
        dma((8,)), dma((8,)), dma((7, 2, 3)), dma((7, 2, 3)),
        dma((4,)), dma((4,)), dma((4,)), dma((4,)),
        dma((7, 2, 3)), dma((7, 2, 3)), dma((8, 2)), dma((8, 2)),
        dma((8,)), dma((8,)), dma, dma,
        dma((3, 2)), dma((3, 2)), dma, dma, dma, dma, dma((3,)), dma((3,)),
    ]
    hidden, dq, dk, dv, ng, nmo, par, gw = pl.pallas_call(
        kernel,
        out_shape=[
            shape((R, 4096)), shape((2, 8, 2, R, HEAD)), shape((1024, HEAD)), shape((1024, HEAD)),
            shape((128, 512), F32), shape((128, 512), F32), shape((128, 4096)), shape((2, 128, 2048)),
        ],
        in_specs=[any_spec] * 5 + [pl.BlockSpec(memory_space=pltpu.VMEM)] + [any_spec] * 5,
        out_specs=[any_spec] * 8,
        scratch_shapes=scratch,
        compiler_params=pltpu.CompilerParams(
            collective_id=0, has_side_effects=True, vmem_limit_bytes=58 << 20
        ),
        cost_estimate=pl.CostEstimate(flops=5 * 10**9, bytes_accessed=12 << 20, transcendentals=10**6),
        name="whole_step",
    )(
        query.reshape(2, 8, 2, R, HEAD), key, value, resid, w_out[0], gain, grad_norm, grad_resid,
        delta[0], global_w, momentum,
    )
    hidden, dq, dk, dv, nw, nm1, nm2, ng, nmo, par = pl.pallas_call(
        finish,
        out_shape=[
            shape((R, 4096)), shape((2, 8, 2, R, HEAD)), shape((1024, HEAD)), shape((1024, HEAD)),
            shape((128, 4096)), shape((128, 4096)), shape((128, 4096)),
            shape((128, 512), F32), shape((128, 512), F32), shape((128, 4096)),
        ],
        in_specs=[any_spec] * 11,
        out_specs=[any_spec] * 10,
        scratch_shapes=[
            vm((2, 128, 2048)), vm((128, 4096)), vm((128, 4096)), vm((128, 4096)),
            vm((128, 4096)), vm((R, 4096)), vm((2, 8, 2, R, HEAD)), vm((1024, HEAD)), vm((1024, HEAD)),
            vm((128, 512), F32), vm((128, 512), F32), dma((27,)), dma((19,)),
        ],
        compiler_params=pltpu.CompilerParams(vmem_limit_bytes=58 << 20),
        cost_estimate=pl.CostEstimate(flops=10**7, bytes_accessed=12 << 20, transcendentals=10**6),
        name="finish",
    )(hidden, dq, dk, dv, ng, nmo, par, gw, w_out[0], moment_one[0], moment_two[0])
    return (
        hidden, dq.reshape(1024, HEAD), dk, dv, nw[None], nm1[None], nm2[None], ng, nmo, par,
    )


def solution(mesh):
    return jax.shard_map(
        per_device,
        mesh=mesh,
        in_specs=(
            P("island", "tp"),
            P("island", "tp"),
            P("island", "tp"),
            P(("island", "tp"), None),
            P("island", "tp", None),
            P("island", None),
            P(("island", "tp"), None),
            P(("island", "tp"), None),
            P("island", "tp", None),
            P("island", "tp", None),
            P("island", "tp", None),
            P("tp", "island"),
            P("tp", "island"),
        ),
        out_specs=(
            P(("island", "tp"), None),
            P("island", "tp"),
            P("island", "tp"),
            P("island", "tp"),
            P("island", "tp", None),
            P("island", "tp", None),
            P("island", "tp", None),
            P("tp", "island"),
            P("tp", "island"),
            P("tp", None),
        ),
        check_vma=False,
    )
```

```python
import functools

import jax
import jax.numpy as jnp
from jax import lax
from jax.experimental import pallas as pl
from jax.experimental.pallas import tpu as pltpu
from jax.sharding import PartitionSpec as P

HEAD = 128
SCALE = HEAD ** (-0.5)
MESH = pl.DeviceIdType.MESH
F32 = jnp.float32
BF16 = jnp.bfloat16
NZ = 8
NY = 4
QZ = 896
QX = 2048 - QZ
SPAN = (slice(0, QZ), slice(QZ, 2048))
R = 32


def f32(a):
    return a.astype(F32)


def dot(a, b):
    return lax.dot_general(a, b, (((1,), (0,)), ((), ())), preferred_element_type=F32)


def dot_nt(a, b):
    return lax.dot_general(a, b, (((1,), (1,)), ((), ())), preferred_element_type=F32)


def dot_tn(a, b):
    return lax.dot_general(a, b, (((0,), (0,)), ((), ())), preferred_element_type=F32)


def kernel(
    q_in, k_in, v_in, resid_in, w_in, gain_ref, gn_in, gr_in, d_in, gl_in, mo_in,
    hid_out, dq_out, dk_out, dv_out, ng_out, nmo_out, par_out, gw_out,
    q4, kv, vv, wp, res, gnv, grv, glv, mov,
    qs, prs, ctx, part0, part1, xrecv, rbuf0, rbuf1, zbuf, xbuf, fin0, fin1, gq0, gq1, G0, G1,
    gco, gcs, gcr, gwacc, gws, gwo, dkacc, dvacc, yrecv, hbuf, xlrecv,
    hidv, dqv, dkv, dvv, ngv, nmov, pbuf,
    ld, od, ctx_s, ctx_r, w_s, w_r, xe_s, xe_r, ring_s, ring_r, fin_s, fin_r,
    a0_s, a0_r, ag_s, ag_r, xf_s, xf_r, gc_s, gc_r, gw_s, gw_r,
    ia_s, ia_r, ib_s, ib_r, ic_s, ic_r, id_s, id_r,
):
    isl = lax.axis_index("island")
    tp = lax.axis_index("tp")
    y, xl = isl // 2, lax.rem(isl, 2)
    xh, z, c = tp // 16, lax.rem(tp // 2, NZ), lax.rem(tp, 2)
    oc, oh = 1 - c, 1 - xh

    def tp_dev(a, b, d):
        return (isl, a * 16 + b * 2 + d)

    sib = tp_dev(xh, z, oc)
    opp = tp_dev(oh, z, c)
    opx = tp_dev(oh, z, oc)
    up = tp_dev(xh, lax.rem(z + 1, NZ), c)
    down = tp_dev(xh, lax.rem(z + NZ - 1, NZ), c)
    nxt = (up, down)
    ypeer = [(lax.rem(y + o, NY) * 2 + xl, tp) for o in (1, 2, 3)]
    xlpeer = (y * 2 + 1 - xl, tp)

    def rc(src, dst, ss, rs, dev):
        return pltpu.make_async_remote_copy(
            src_ref=src, dst_ref=dst, send_sem=ss, recv_sem=rs, device_id=dev, device_id_type=MESH
        )

    def cols(ref, at, width):
        return ref.at[:, pl.ds(pl.multiple_of(at * width, width), width)]

    loads = {}

    def load(name, src, dst):
        cp = pltpu.make_async_copy(src, dst, ld.at[len(loads)])
        loads[name] = cp
        cp.start()

    load("q", q_in, q4)
    load("k", k_in, kv)
    load("v", v_in, vv)
    load("wp", cols(w_in, c, 2048), wp.at[0])

    barrier = pltpu.get_barrier_semaphore()
    partners = [sib, opp, opx, up, down, xlpeer] + ypeer
    for dev in partners:
        pl.semaphore_signal(barrier, inc=1, device_id=dev, device_id_type=MESH)

    def places(g):
        return lax.rem(z - g + NZ, NZ), lax.rem(z + g, NZ)

    def ctx_copy(g):
        return rc(ctx.at[g, 0], ctx.at[g, 1], ctx_s.at[g], ctx_r.at[g], sib)

    def xe_copy(g):
        return rc(part1.at[g, oh], xrecv.at[g], xe_s.at[g], xe_r.at[g], opp)

    def attend(g):
        s0, s1 = places(g)
        qu = jnp.concatenate([q4[0, s0, 0], q4[0, s1, 1], q4[1, s0, 0], q4[1, s1, 1]], axis=0)
        qs[g] = qu
        scores = dot_nt(qu, kv[...]) * SCALE
        row = lax.broadcasted_iota(jnp.int32, (4 * R, 1), 0)
        odd = lax.rem(row // R, 2)
        qpos = (row // (2 * R)) * 512 + odd * R + lax.rem(row, R) + 64 * (s0 + odd * (s1 - s0))
        kpos = lax.broadcasted_iota(jnp.int32, (4 * R, 1024), 1)
        scores = jnp.where(kpos <= qpos, scores, -1e30)
        expo = jnp.exp(scores - jnp.max(scores, axis=1, keepdims=True))
        probs = (expo * (1.0 / jnp.sum(expo, axis=1, keepdims=True))).astype(BF16)
        prs[g] = probs
        ctx[g, 0] = dot(probs, vv[...]).astype(BF16)

    def both(g):
        return jnp.concatenate([ctx[g, 0], ctx[g, 1]], axis=1)

    def project(g, order=(1, 0)):
        ctx_copy(g).wait_recv()
        cx = both(g)
        for t in order:
            wt = wp[:, :, SPAN[t]].reshape(256, -1)
            out = dot(cx, wt).astype(BF16).reshape(2, 2, R, -1)
            if t == 1:
                part1[g] = out
                xe_copy(g).start()
            else:
                part0[g] = out

    halves = (oh, xh, xh)

    def ring_copy(k, p, j):
        if j < 2:
            src, dst = part0.at[k + 1, halves[j], p], rbuf0.at[k, p, j]
        else:
            src, dst = part1.at[k + 1, xh, p], rbuf1.at[k, p]
        return rc(src, dst, ring_s.at[k, p, j], ring_r.at[k, p, j], nxt[p])

    def z_step(k, j, first=False):
        h = halves[j]
        for p in range(2):
            if not first:
                ring_copy(k - 1, p, j).wait_recv()
                part0[k + 1, h, p] = (f32(part0[k + 1, h, p]) + f32(rbuf0[k - 1, p, j])).astype(BF16)
            ring_copy(k, p, j).start()

    def x_step(k, first=False):
        xe_copy(k + 1).wait_recv()
        for p in range(2):
            total = f32(part1[k + 1, xh, p]) + f32(xrecv[k + 1, p])
            if not first:
                ring_copy(k - 1, p, 2).wait_recv()
                total = total + f32(rbuf1[k - 1, p])
            part1[k + 1, xh, p] = total.astype(BF16)
            ring_copy(k, p, 2).start()

    ib_copy = rc(hbuf, xlrecv, ib_s, ib_r, xlpeer)
    ic_copy = rc(pbuf.at[y, xl], pbuf.at[y, xl], ic_s, ic_r, xlpeer)
    id_copies = [rc(pbuf.at[y], pbuf.at[y], id_s.at[o], id_r.at[o], ypeer[o]) for o in range(3)]

    def over_y(e):
        return f32(yrecv[0, e]) + f32(yrecv[1, e]) + f32(yrecv[2, e]) + f32(yrecv[3, e])

    def outer_b():
        for cp in a_copies:
            cp.wait_recv()
        loads["d0"].wait()
        loads["d1"].wait()
        hbuf[...] = over_y(1 - xl).astype(BF16)
        ib_copy.start()

    def outer_c():
        ib_copy.wait_recv()
        loads["gl"].wait()
        loads["mo"].wait()
        average = (over_y(xl) + f32(xlrecv[...])) * 0.125
        moment = 0.9 * mov[...] + average
        new = glv[...] - 0.7 * (average + 0.9 * moment)
        nmov[...] = moment
        ngv[...] = new
        pbuf[y, xl] = new.astype(BF16)
        ic_copy.start()

    def outer_d():
        ic_copy.wait_recv()
        for cp in id_copies:
            cp.start()

    loads["q"].wait()
    loads["k"].wait()
    loads["v"].wait()
    attend(1)
    pl.semaphore_wait(barrier, len(partners))
    w_copy = rc(cols(w_in, oc, 2048), wp.at[1], w_s, w_r, sib)
    w_copy.start()
    ctx_copy(1).start()
    a_copies = []
    for o in range(3):
        ny = lax.rem(y + o + 1, NY)
        for e in range(2):
            cp = rc(cols(d_in, ny * 2 + e, 512), yrecv.at[y, e], ia_s.at[o, e], ia_r.at[o, e], ypeer[o])
            cp.start()
            a_copies.append(cp)
    for e in range(2):
        load(f"d{e}", cols(d_in, y * 2 + e, 512), yrecv.at[y, e])
    for e in range(2):
        load(f"res{e}", resid_in.at[:, e * 2048 : (e + 1) * 2048], res.at[e])
        load(f"gn{e}", gn_in.at[:, e * 2048 : (e + 1) * 2048], gnv.at[e])
        load(f"gr{e}", gr_in.at[:, e * 2048 : (e + 1) * 2048], grv.at[e])
    load("gl", gl_in, glv)
    load("mo", mo_in, mov)
    attend(2)
    ctx_copy(2).start()
    loads["wp"].wait()
    w_copy.wait_recv()
    project(1, order=(0, 1))
    z_step(0, 0, first=True)
    z_step(0, 1, first=True)
    attend(3)
    ctx_copy(3).start()
    project(2)
    attend(4)
    ctx_copy(4).start()
    project(3)

    z_step(1, 0)
    attend(5)
    ctx_copy(5).start()
    z_step(1, 1)
    x_step(0, first=True)
    project(4)

    def forward(k, carry):
        z_step(k, 0)

        @pl.when(k <= 4)
        def _():
            g = lax.rem(k + 4, NZ)
            attend(g)
            ctx_copy(g).start()

        z_step(k, 1)
        x_step(k - 1)

        @pl.when(k <= 5)
        def _():
            project(lax.rem(k + 3, NZ))

        @pl.when(k == 3)
        def _():
            outer_b()

        @pl.when(k == 5)
        def _():
            outer_c()

        return carry

    lax.fori_loop(2, 7, forward, 0)

    fin_copies = [
        rc(zbuf.at[xh, oc], fin0.at[0], fin_s.at[0], fin_r.at[0], sib),
        rc(zbuf.at[oh, c], fin0.at[1], fin_s.at[1], fin_r.at[1], opp),
        rc(zbuf.at[oh, oc], fin0.at[2], fin_s.at[2], fin_r.at[2], opx),
        rc(xbuf.at[oc], fin1, fin_s.at[3], fin_r.at[3], sib),
    ]

    def z_last(j):
        for p in range(2):
            ring_copy(6, p, j).wait_recv()
            zbuf[halves[j], p] = (f32(part0[0, halves[j], p]) + f32(rbuf0[6, p, j])).astype(BF16)

    z_last(0)
    fin_copies[1].start()
    fin_copies[2].start()
    x_step(6)
    z_last(1)
    fin_copies[0].start()
    xe_copy(0).wait_recv()
    for p in range(2):
        ring_copy(6, p, 2).wait_recv()
        xbuf[p] = (f32(part1[0, xh, p]) + f32(xrecv[0, p]) + f32(rbuf1[6, p])).astype(BF16)
    fin_copies[3].start()
    for e in range(2):
        for name in ("res", "gn", "gr"):
            loads[f"{name}{e}"].wait()
    fin_copies[0].wait_recv()
    fin_copies[3].wait_recv()
    fin_copies[1].wait_recv()
    fin_copies[2].wait_recv()

    def of_block(cc, t):
        if t == 0:
            if cc is c:
                return f32(zbuf[xh, c]) + f32(fin0[1])
            return f32(fin0[0]) + f32(fin0[2])
        return f32(xbuf[c]) if cc is c else f32(fin1[...])

    blocks = [(oc, 1), (oc, 0), (c, 0), (c, 1)]
    low = c == 0
    values, scaleds = [], []
    square = jnp.zeros((R, 1), F32)
    cross = jnp.zeros((R, 1), F32)
    for cc, t in blocks:
        at = SPAN[t]
        hid = (f32(res[cc, :, at]) + of_block(cc, t)).astype(BF16)
        hidv[cc, :, at] = hid
        val = f32(hid)
        first_half = low if cc is c else jnp.logical_not(low)
        gain = jnp.where(
            first_half, f32(gain_ref[:, at]), f32(gain_ref[:, at.start + 2048 : at.stop + 2048])
        )
        scaled = f32(gnv[cc, :, at]) * gain
        square = square + jnp.sum(val * val, axis=1, keepdims=True)
        cross = cross + jnp.sum(scaled * val, axis=1, keepdims=True)
        values.append(val)
        scaleds.append(scaled)
    rstd = lax.rsqrt(square * (1.0 / 4096) + 1e-05)
    inner = cross * rstd * (1.0 / 4096)
    a0_copies = [
        rc(gq0.at[1], G0.at[0, xh, c], a0_s.at[0], a0_r.at[0], sib),
        rc(gq1, G1.at[0, xh, c], a0_s.at[1], a0_r.at[1], sib),
        rc(gq0.at[0], G0.at[0, xh, c], a0_s.at[2], a0_r.at[2], opp),
        rc(gq0.at[1], G0.at[0, xh, c], a0_s.at[3], a0_r.at[3], opx),
    ]
    for (cc, t), val, scaled in zip(blocks, values, scaleds):
        back = (f32(grv[cc, :, SPAN[t]]) + rstd * (scaled - val * rstd * inner)).astype(BF16)
        if t == 1 and cc is oc:
            gq1[...] = back
            a0_copies[1].start()
        elif t == 1:
            G1[0, xh, c] = back
        elif cc is oc:
            gq0[1] = back
            a0_copies[3].start()
            a0_copies[0].start()
        else:
            gq0[0] = back
            a0_copies[2].start()
            G0[0, xh, c] = back

    outs = []

    def emit(src, dst):
        cp = pltpu.make_async_copy(src, dst, od.at[len(outs)])
        outs.append(cp)
        cp.start()

    def ag_copy(k, p, j):
        if j == 2:
            src, dst = G1.at[k, xh, p], G1.at[k + 1, xh, p]
        else:
            h = (xh, oh)[j]
            src, dst = G0.at[k, h, p], G0.at[k + 1, h, p]
        return rc(src, dst, ag_s.at[k, p, j], ag_r.at[k, p, j], nxt[p])

    def xf_copy(g, p):
        return rc(G1.at[g, xh, p], G1.at[g, xh, p], xf_s.at[g, p], xf_r.at[g, p], opp)

    def lead(k, last=False):
        for p in range(2):
            ag_copy(k, p, 2).wait_recv()
            if not last:
                ag_copy(k + 1, p, 2).start()
            xf_copy(k + 1, p).start()

    a0_copies[1].wait_recv()
    for p in range(2):
        ag_copy(0, p, 2).start()
        xf_copy(0, p).start()
    a0_copies[0].wait_recv()
    for p in range(2):
        ag_copy(0, p, 0).start()
    gwacc[...] = jnp.zeros_like(gwacc)
    dkacc[...] = jnp.zeros_like(dkacc)
    dvacc[...] = jnp.zeros_like(dvacc)
    a0_copies[2].wait_recv()
    a0_copies[3].wait_recv()
    for p in range(2):
        ag_copy(0, p, 1).start()
    lead(0)
    for e in range(2):
        emit(hidv.at[e], hid_out.at[:, e * 2048 : (e + 1) * 2048])
    emit(ngv, ng_out)
    emit(nmov, nmo_out)

    def weigh(g, last=False):
        for p in range(2):
            xf_copy(g, p).wait_recv()
        cx = both(g)
        gc = None
        for t, G in enumerate((G0, G1)):
            piece = dot_nt(G[g].reshape(4 * R, -1), wp[:, :, SPAN[t]].reshape(256, -1))
            gc = piece if gc is None else gc + piece
        gco[g] = gc[:, :HEAD]
        gcs[g] = gc[:, HEAD:]
        gc_copy(g).start()
        for t, G in enumerate((G0, G1)):
            total = gwacc[:, SPAN[t]] + dot_tn(cx, G[g].reshape(4 * R, -1))
            if last:
                gws[:, SPAN[t]] = total[HEAD:].astype(BF16)
                gwo[:, SPAN[t]] = total[:HEAD].astype(BF16)
            else:
                gwacc[:, SPAN[t]] = total

    def gc_copy(g):
        return rc(gcs.at[g], gcr.at[g], gc_s.at[g], gc_r.at[g], sib)

    def attend_back(g):
        gc_copy(g).wait_recv()
        s0, s1 = places(g)
        gc = (gco[g] + gcr[g]).astype(BF16)
        probs = prs[g]
        row_dot = jnp.sum(f32(gc) * f32(ctx[g, 0]), axis=1, keepdims=True)
        gs = (f32(probs) * (dot_nt(gc, vv[...]) - row_dot)).astype(BF16)
        dq = (dot(gs, kv[...]) * SCALE).astype(BF16)
        for h in range(2):
            for p, s in enumerate((s0, s1)):
                dqv[h, s, p] = dq[(2 * h + p) * R : (2 * h + p + 1) * R]
        dkacc[...] += dot_tn(gs, qs[g])
        dvacc[...] += dot_tn(probs, gc)

    def follow(k, j):
        for p in range(2):
            ag_copy(k, p, j).wait_recv()
            ag_copy(k + 1, p, j).start()

    def drain(k):
        for p in range(2):
            for j in range(3):
                ring_copy(k, p, j).wait_send()
        ctx_copy(k).wait_send()
        xe_copy(k).wait_send()

    def backward(k, carry):
        follow(k, 0)
        weigh(k)
        follow(k, 1)

        @pl.when(k < 5)
        def _():
            lead(k + 1)

        @pl.when(k == 5)
        def _():
            lead(6, last=True)

        @pl.when(k >= 1)
        def _():
            attend_back(k - 1)

        @pl.when(k == 1)
        def _():
            outer_d()

        drain(k)
        return carry

    lax.fori_loop(0, 6, backward, 0)
    weigh(6)
    attend_back(5)
    for cp in id_copies:
        cp.wait_recv()
    for i in range(8):
        emit(pbuf.at[i // 2, i % 2], par_out.at[:, i * 512 : (i + 1) * 512])
    attend_back(6)
    drain(6)
    ctx_copy(7).wait_send()
    xe_copy(7).wait_send()
    w_copy.wait_send()
    for cp in a_copies + fin_copies + a0_copies + id_copies + [ib_copy, ic_copy]:
        cp.wait_send()

    def drain_back(k, carry):
        for p in range(2):
            for j in range(3):
                ag_copy(k, p, j).wait_send()
            xf_copy(k, p).wait_send()
        gc_copy(k).wait_send()
        return carry

    lax.fori_loop(0, 6, drain_back, 0)
    for j in range(2):
        for p in range(2):
            ag_copy(6, p, j).wait_recv()
    weigh(7, last=True)
    gw_copy = rc(gws, gw_out.at[c], gw_s, gw_r, sib)
    gw_copy.start()
    emit(gwo, gw_out.at[c])
    attend_back(7)
    emit(dqv, dq_out)
    dkv[...] = (dkacc[...] * SCALE).astype(BF16)
    emit(dkv, dk_out)
    dvv[...] = dvacc[...].astype(BF16)
    emit(dvv, dv_out)

    drain_back(6, 0)
    for p in range(2):
        xf_copy(7, p).wait_send()
    gc_copy(7).wait_send()
    gw_copy.wait_send()
    gw_copy.wait_recv()
    for cp in outs:
        cp.wait()


def finish(
    hid_in, dq_in, dk_in, dv_in, ng_in, nmo_in, par_in, gw_in, w_in, m1_in, m2_in,
    hid_out, dq_out, dk_out, dv_out, nw_out, nm1_out, nm2_out, ng_out, nmo_out, par_out,
    gw, w, m1, m2, par, hid, dq, dk, dv, ng, nmo, ld, od,
):
    outs, loads = [], []

    def emit(src, dst):
        cp = pltpu.make_async_copy(src, dst, od.at[len(outs)])
        outs.append(cp)
        cp.start()

    def load(src, dst):
        cp = pltpu.make_async_copy(src, dst, ld.at[len(loads)])
        loads.append(cp)
        cp.start()

    for i in range(4):
        rows = slice(i * 32, (i + 1) * 32)
        for e in range(2):
            load(gw_in.at[e, rows], gw.at[e, rows])
        load(m1_in.at[rows], m1.at[rows])
        load(m2_in.at[rows], m2.at[rows])
        load(w_in.at[rows], w.at[rows])
    passed = (
        (hid_in, hid, hid_out), (dq_in, dq, dq_out), (dk_in, dk, dk_out), (dv_in, dv, dv_out),
        (ng_in, ng, ng_out), (nmo_in, nmo, nmo_out), (par_in, par, par_out),
    )
    for src, mid, _ in passed:
        load(src, mid)
    for i in range(4):
        for cp in loads[5 * i : 5 * i + 5]:
            cp.wait()
        for rows in (slice(i * 32, i * 32 + 16), slice(i * 32 + 16, i * 32 + 32)):
            for e in range(2):
                at = slice(e * 2048, (e + 1) * 2048)
                grad = f32(gw[e, rows])
                first = 0.9 * f32(m1[rows, at]) + 0.1 * grad
                second = 0.95 * f32(m2[rows, at]) + 0.05 * grad * grad
                update = (first * (1.0 / (1.0 - 0.9**10))) / (
                    jnp.sqrt(second * (1.0 / (1.0 - 0.95**10))) + 1e-08
                )
                w[rows, at] = (f32(w[rows, at]) - 0.001 * update).astype(BF16)
                m1[rows, at] = first.astype(BF16)
                m2[rows, at] = second.astype(BF16)
        rows = slice(i * 32, (i + 1) * 32)
        for src, dst in ((w, nw_out), (m1, nm1_out), (m2, nm2_out)):
            emit(src.at[rows], dst.at[rows])
        for at in (2 * i, 2 * i + 1):
            if at < len(passed):
                loads[20 + at].wait()
                emit(passed[at][1], passed[at][2])
    for cp in outs:
        cp.wait()


def per_device(
    query, key, value, resid, w_out, gain, grad_norm, grad_resid, moment_one, moment_two,
    delta, global_w, momentum,
):
    any_spec = pl.BlockSpec(memory_space=pl.ANY)
    dma = pltpu.SemaphoreType.DMA

    def vm(shape, dtype=BF16):
        return pltpu.VMEM(shape, dtype)

    def shape(dims, dtype=BF16):
        return jax.ShapeDtypeStruct(dims, dtype)

    scratch = [
        vm((2, 8, 2, R, HEAD)), vm((1024, HEAD)), vm((1024, HEAD)),
        vm((2, 128, 2048)), vm((2, R, 2048)), vm((2, R, 2048)), vm((2, R, 2048)),
        vm((128, 512), F32), vm((128, 512), F32),
        vm((8, 128, HEAD)), vm((8, 128, 1024)), vm((8, 2, 128, HEAD)),
        vm((8, 2, 2, R, QZ)), vm((8, 2, 2, R, QX)), vm((8, 2, R, QX)),
        vm((7, 2, 2, R, QZ)), vm((7, 2, R, QX)),
        vm((2, 2, R, QZ)), vm((2, R, QX)), vm((3, R, QZ)), vm((R, QX)),
        vm((2, R, QZ)), vm((R, QX)), vm((8, 2, 2, R, QZ)), vm((8, 2, 2, R, QX)),
        vm((8, 128, HEAD), F32), vm((8, 128, HEAD), F32), vm((8, 128, HEAD), F32),
        vm((256, 2048), F32), vm((128, 2048)), vm((128, 2048)),
        vm((1024, HEAD), F32), vm((1024, HEAD), F32),
        vm((4, 2, 128, 512)), vm((128, 512)), vm((128, 512)),
        vm((2, R, 2048)), vm((2, 8, 2, R, HEAD)), vm((1024, HEAD)), vm((1024, HEAD)),
        vm((128, 512), F32), vm((128, 512), F32), vm((4, 2, 128, 512)),
        dma((14,)), dma((16,)), dma((8,)), dma((8,)), dma, dma,
        dma((8,)), dma((8,)), dma((7, 2, 3)), dma((7, 2, 3)),
        dma((4,)), dma((4,)), dma((4,)), dma((4,)),
        dma((7, 2, 3)), dma((7, 2, 3)), dma((8, 2)), dma((8, 2)),
        dma((8,)), dma((8,)), dma, dma,
        dma((3, 2)), dma((3, 2)), dma, dma, dma, dma, dma((3,)), dma((3,)),
    ]
    hidden, dq, dk, dv, ng, nmo, par, gw = pl.pallas_call(
        kernel,
        out_shape=[
            shape((R, 4096)), shape((2, 8, 2, R, HEAD)), shape((1024, HEAD)), shape((1024, HEAD)),
            shape((128, 512), F32), shape((128, 512), F32), shape((128, 4096)), shape((2, 128, 2048)),
        ],
        in_specs=[any_spec] * 5 + [pl.BlockSpec(memory_space=pltpu.VMEM)] + [any_spec] * 5,
        out_specs=[any_spec] * 8,
        scratch_shapes=scratch,
        compiler_params=pltpu.CompilerParams(
            collective_id=0, has_side_effects=True, vmem_limit_bytes=58 << 20
        ),
        cost_estimate=pl.CostEstimate(flops=5 * 10**9, bytes_accessed=12 << 20, transcendentals=10**6),
        name="whole_step",
    )(
        query.reshape(2, 8, 2, R, HEAD), key, value, resid, w_out[0], gain, grad_norm, grad_resid,
        delta[0], global_w, momentum,
    )
    hidden, dq, dk, dv, nw, nm1, nm2, ng, nmo, par = pl.pallas_call(
        finish,
        out_shape=[
            shape((R, 4096)), shape((2, 8, 2, R, HEAD)), shape((1024, HEAD)), shape((1024, HEAD)),
            shape((128, 4096)), shape((128, 4096)), shape((128, 4096)),
            shape((128, 512), F32), shape((128, 512), F32), shape((128, 4096)),
        ],
        in_specs=[any_spec] * 11,
        out_specs=[any_spec] * 10,
        scratch_shapes=[
            vm((2, 128, 2048)), vm((128, 4096)), vm((128, 4096)), vm((128, 4096)),
            vm((128, 4096)), vm((R, 4096)), vm((2, 8, 2, R, HEAD)), vm((1024, HEAD)), vm((1024, HEAD)),
            vm((128, 512), F32), vm((128, 512), F32), dma((27,)), dma((19,)),
        ],
        compiler_params=pltpu.CompilerParams(vmem_limit_bytes=58 << 20),
        cost_estimate=pl.CostEstimate(flops=10**7, bytes_accessed=12 << 20, transcendentals=10**6),
        name="finish",
    )(hidden, dq, dk, dv, ng, nmo, par, gw, w_out[0], moment_one[0], moment_two[0])
    return (
        hidden, dq.reshape(1024, HEAD), dk, dv, nw[None], nm1[None], nm2[None], ng, nmo, par,
    )


def solution(mesh):
    return jax.shard_map(
        per_device,
        mesh=mesh,
        in_specs=(
            P("island", "tp"),
            P("island", "tp"),
            P("island", "tp"),
            P(("island", "tp"), None),
            P("island", "tp", None),
            P("island", None),
            P(("island", "tp"), None),
            P(("island", "tp"), None),
            P("island", "tp", None),
            P("island", "tp", None),
            P("island", "tp", None),
            P("tp", "island"),
            P("tp", "island"),
        ),
        out_specs=(
            P(("island", "tp"), None),
            P("island", "tp"),
            P("island", "tp"),
            P("island", "tp"),
            P("island", "tp", None),
            P("island", "tp", None),
            P("island", "tp", None),
            P("tp", "island"),
            P("tp", "island"),
            P("tp", None),
        ),
        check_vma=False,
    )
```
